32 devices in a mesh: rep: 4 (over y, core), ep: 8 (over z, x).
Axes of the slice: x: 2, y: 2, z: 4, core: 2. Of those that a mesh axis runs over, the one named last changes fastest.
Arguments:
- tokens: bfloat16 [4096, 2048], P(('rep', 'ep')), may hold values from -6 to 6
- norm_gain: float32 [2048], replicated, may hold values from 0.5 to 1.5
- gates: float32 [4096], P(('rep', 'ep')), may hold values from 0.25 to 1
- expert_ids: int32 [4096], P(('rep', 'ep')), may hold values from 0 to 7, as said below
- slots: int32 [4096], P(('rep', 'ep')), may hold values from 0 to 15, as said below
- dropped: int32 [4096], P(('rep', 'ep')), may hold values from 0 to 1
- res_in: bfloat16 [2048, 4096], P('ep', 'rep'), may hold values from -0.125 to 0.125
- res_out: bfloat16 [4096, 2048], P('rep', 'ep'), may hold values from -0.09375 to 0.09375
- expert_in: bfloat16 [8, 2048, 4096], P('ep', None, 'rep'), may hold values from -0.125 to 0.125
- expert_out: bfloat16 [8, 4096, 2048], P('ep', 'rep'), may hold values from -0.09375 to 0.09375
Outputs:
- mixed: bfloat16 [4096, 2048], P(('rep', 'ep'))
The draws below stay inside these ranges and needn't reach their ends.
Inputs may be any that keep to these rules, and one draw needn't show every extreme that they name: `expert_ids`: within the tokens of one device, two tokens with the same expert and dropped = 0 have different slots; slots count such tokens in order, and a token is dropped exactly when 16 earlier tokens of its device chose its expert. In every draw some expert receives at least 2 tokens from every device. `slots`: slot of a dropped token is 0.
All inputs are finite; a program needn't handle non-finite values.
Results may differ from the reference program's by a relative error of at most 0.0045.
Values may be sent and summed in bfloat16 or wider, within the bound.
A program may use at most 128 MiB of HBM per device.

```python
import math
import jax
import jax.numpy as jnp
from jax import lax

D = 2048
EH = 4096
RH = 4096
TOK_DEV = 128
EXPERTS = 8
CAP = 16
TOKENS = 4096


def route_table(key):
    devices = TOKENS // TOK_DEV
    first, second = jax.random.split(key)
    choices_drawn = jax.random.randint(first, (devices, TOK_DEV), 0, EXPERTS)
    shared = jax.random.randint(second, (), 0, EXPERTS)
    choices_drawn = choices_drawn.at[:, 0].set(shared).at[:, 1].set(shared)
    places = jnp.arange(TOK_DEV)
    earlier = (choices_drawn[:, :, None] == choices_drawn[:, None, :]) & (places[:, None] > places[None, :])[None]
    ranks = jnp.sum(earlier.astype(jnp.int32), axis=2).astype(jnp.int32)
    return (choices_drawn.astype(jnp.int32), ranks)


def draw_expert_ids(key, part):
    chosen, ranks = route_table(key)
    return chosen.reshape(-1)


def draw_slots(key, part):
    chosen, ranks = route_table(key)
    return jnp.where(ranks < CAP, ranks, 0).astype(jnp.int32).reshape(-1)


def draw_dropped(key, part):
    chosen, ranks = route_table(key)
    return (ranks >= CAP).astype(jnp.int32).reshape(-1)


def steps_of(own_key, shape, cuts, low, top_value):
    def one(axis_at, blocks):
        steps = jax.random.uniform(jax.random.fold_in(jax.random.fold_in(own_key, 6), axis_at), (blocks,), jnp.float32, low / len(cuts), top_value / len(cuts))
        return jnp.repeat(jnp.exp(steps), shape[axis_at] // blocks).reshape((-1,) + (1,) * (len(shape) - axis_at - 1))

    factor_of = one(*cuts[0])
    for cut in cuts[1:]:
        factor_of = factor_of * one(*cut)
    return factor_of


def centred(own_key, shape, width, limit, pieces=(), held_as=jnp.bfloat16):
    entries = jax.random.normal(own_key, shape, jnp.float32) * width
    if len(pieces) > 0:
        entries = steps_of(own_key, shape, pieces, -0.22, 0.18) * entries
    return jnp.clip(entries, min=-limit, max=limit).astype(held_as)


def setup_inputs(seed: int = 0) -> dict:
    arg_keys = jax.random.split(jax.random.key(seed), 11)
    tokens = centred(arg_keys[0], (TOKENS, D), 1.0, 6.0, ((0, 32),))
    norm_gain = jnp.clip(1.0 + 0.1 * jax.random.normal(arg_keys[1], (D,), jnp.float32), 0.5, 1.5)
    gates = jnp.clip(jnp.exp(math.log(1.0) - 1.3862944 * jax.random.uniform(arg_keys[2], (TOKENS,), jnp.float32) ** steps_of(arg_keys[2], (TOKENS,), ((0, 32),), -0.2, 0.2)), 0.25, 1.0)
    expert_ids = draw_expert_ids(jax.random.fold_in(arg_keys[10], 71), 0)
    slots = draw_slots(jax.random.fold_in(arg_keys[10], 71), 0)
    dropped = draw_dropped(jax.random.fold_in(arg_keys[10], 71), 0)
    res_in = centred(arg_keys[6], (D, RH), D ** -0.5, 0.125, ((0, 8), (1, 4)))
    res_out = centred(arg_keys[7], (RH, D), RH ** -0.5, 0.09375, ((0, 4), (1, 8)))
    expert_in = centred(arg_keys[8], (EXPERTS, D, EH), D ** -0.5, 0.125, ((0, 8), (2, 4)))
    expert_out = centred(arg_keys[9], (EXPERTS, EH, D), EH ** -0.5, 0.09375, ((0, 8), (1, 4)))
    return {"tokens": tokens, "norm_gain": norm_gain, "gates": gates, "expert_ids": expert_ids, "slots": slots, "dropped": dropped, "res_in": res_in, "res_out": res_out, "expert_in": expert_in, "expert_out": expert_out}


def rms_norm(tokens, norm_gain):
    values = tokens.astype(jnp.float32)
    scale = lax.rsqrt(lax.optimization_barrier(jnp.mean(values * values, axis=-1, keepdims=True)) + 1e-06)
    return (values * scale * norm_gain).astype(jnp.bfloat16)

def mlp_rows(rows, first, second):
    hidden = jax.nn.gelu(jnp.dot(rows, first, preferred_element_type=jnp.float32), approximate=True).astype(jnp.bfloat16)
    return jnp.dot(hidden, second, preferred_element_type=jnp.float32)

def reference(tokens, norm_gain, gates, expert_ids, slots, dropped, res_in, res_out, expert_in, expert_out):
    normed = rms_norm(tokens, norm_gain)
    devices = TOKENS // TOK_DEV
    owner = (jnp.arange(TOKENS) // TOK_DEV).astype(jnp.int32)
    keep = dropped == 0
    total_slots = EXPERTS * devices * CAP
    index = jnp.where(keep, expert_ids * (devices * CAP) + owner * CAP + slots, total_slots).astype(jnp.int32)
    buffer = jnp.zeros((total_slots, D), jnp.bfloat16).at[index].set(normed, mode='drop')
    buffer = buffer.reshape(EXPERTS, devices * CAP, D)
    results = lax.map(lambda item: mlp_rows(item[0], item[1], item[2]), (buffer, expert_in, expert_out))
    picked = jnp.take(results.reshape(total_slots, D), jnp.where(keep, index, 0), axis=0)
    exp_branch = jnp.where(keep[:, None], picked, 0.0)
    blocks = normed.reshape(devices, TOK_DEV, D)
    res_branch = lax.map(lambda rows: mlp_rows(rows, res_in, res_out), blocks).reshape(TOKENS, D)
    mixed = tokens.astype(jnp.float32) + res_branch + gates[:, None] * exp_branch
    return mixed.astype(jnp.bfloat16)
```

```python
import jax
import jax.numpy as jnp
from jax import lax
from jax.experimental import pallas as pl
from jax.experimental.pallas import tpu as pltpu
from jax.sharding import PartitionSpec as P

F32 = jnp.float32
BF16 = jnp.bfloat16
PLANES = 4


def gelu(x):
    return x * (0.5 * (1.0 + jnp.tanh(0.7978845608028654 * (x + 0.044715 * (x * x * x)))))


def dot(a, b):
    return jnp.dot(a, b, preferred_element_type=F32)


def layer_kernel(
    tokens, gain, gates, ids, slots, dropped, res_in, res_out, exp_in, exp_out,
    out,
    w1, w2, ein, eout, normed, xrows, disp, ehid,
    er_send, er_keep, er_recv, ey_send, ey_keep, ey_recv, eb_send, back,
    rhid, pc_send, pc_keep, pc_recv, px_send, px_keep, px_recv, py_send, py_keep, py_recv,
    res,
    local_sem, wx_ssem, wx_rsem, w1_ssem, w1_rsem, w2_ssem, w2_rsem,
    n_ssem, n_rsem, d_ssem, d_rsem, x_ssem, x_rsem, e_ssem, e_rsem, b_ssem, b_rsem,
    r_ssem, r_rsem,
):
    rep, ep = lax.axis_index("rep"), lax.axis_index("ep")
    y, c = rep // 2, rep % 2
    z, x = ep // 2, ep % 2
    rows, width = tokens.shape
    n_ep = 2 * PLANES
    cap = rows // n_ep
    half = w1.shape[1]
    chunk = res_in.shape[0]
    cols = 2 * chunk

    def dev(r, e):
        return {"rep": r, "ep": e}

    core_dev = dev(rep + 1 - 2 * c, ep)
    y_dev = dev(rep + 2 - 4 * y, ep)
    x_dev = dev(rep, ep + 1 - 2 * x)
    up_dev, down_dev = dev(rep, ep + 2), dev(rep, ep - 2)

    def peer(k):
        return lax.rem(ep + k, n_ep)

    def remote(src, dst, ssem, rsem, device):
        return pltpu.make_async_remote_copy(
            src_ref=src, dst_ref=dst, send_sem=ssem, recv_sem=rsem,
            device_id=device, device_id_type=pl.DeviceIdType.MESH,
        )

    def arrived(dst, ssem, rsem):
        remote(dst, dst, ssem, rsem, core_dev).wait_recv()

    sent = []

    def send(src, dst, ssem, rsem, device):
        copy = remote(src, dst, ssem, rsem, device)
        copy.start()
        sent.append(copy)

    def at(i, n):
        return pl.ds(pl.multiple_of(i * n, n), n)

    barrier = pltpu.get_barrier_semaphore()
    for k in range(1, n_ep):
        pl.semaphore_signal(
            barrier, inc=1, device_id=dev(rep, peer(k)), device_id_type=pl.DeviceIdType.MESH
        )
    for device in (core_dev, y_dev):
        pl.semaphore_signal(barrier, inc=1, device_id=device, device_id_type=pl.DeviceIdType.MESH)

    own_w1 = pltpu.make_async_copy(res_in.at[:, at(x, half)], w1.at[at(ep, chunk), :], local_sem.at[0])
    own_w2 = pltpu.make_async_copy(
        res_out.at[at(x, half), :], w2.at[z, :, at(x, chunk)], local_sem.at[1]
    )
    load_in = pltpu.make_async_copy(exp_in, ein, local_sem.at[2])
    load_out = pltpu.make_async_copy(exp_out, eout, local_sem.at[3])
    for copy in (own_w1, own_w2, load_in, load_out):
        copy.start()

    pl.semaphore_wait(barrier, n_ep + 1)

    send(res_in.at[:, at(1 - x, half)], w1.at[at(ep, chunk), :], wx_ssem.at[0], wx_rsem.at[0], x_dev)
    send(
        res_out.at[at(1 - x, half), :], w2.at[z, :, at(x, chunk)],
        wx_ssem.at[1], wx_rsem.at[1], x_dev,
    )

    values = tokens[...].astype(F32)
    scale = lax.rsqrt(jnp.mean(values * values, axis=-1, keepdims=True) + 1e-06)
    own_normed = (values * scale * gain[...]).astype(BF16)

    def n_at(cc, xx, yy):
        return normed.at[at(cc * 4 + xx * 2 + yy, rows), :]

    normed[at(c * 4 + x * 2 + y, rows), :] = own_normed

    target = ids[...] * cap + slots[...]
    places = lax.broadcasted_iota(jnp.int32, (n_ep * cap, rows), 0)
    table = jnp.where((places == target) & (dropped[...] == 0), 1.0, 0.0).astype(BF16)
    disp[...] = dot(table, own_normed).astype(BF16)

    def x_at(cc, yy):
        return xrows.at[at(cc * 2 + yy, rows), :]

    def x_part(cc, yy, e):
        return xrows.at[pl.ds(pl.multiple_of((cc * 2 + yy) * rows + e * cap, cap), cap), :]

    for k in range(1, n_ep):
        send(disp.at[at(peer(k), cap), :], x_part(c, y, ep), d_ssem.at[k], d_rsem.at[k], dev(rep, peer(k)))
    x_part(c, y, ep)[...] = disp[at(ep, cap), :]

    send(n_at(c, x, y), n_at(c, x, y), n_ssem.at[0], n_rsem.at[0], x_dev)
    send(n_at(c, x, y), n_at(c, x, y), n_ssem.at[1], n_rsem.at[1], y_dev)
    send(n_at(c, x, y), n_at(c, x, y), n_ssem.at[2], n_rsem.at[2], core_dev)

    def w1_at(s):
        return w1.at[at(s, cols), :]

    def w2_at(s):
        return w2.at[s]

    inner = (z > 0) & (z < PLANES - 1)

    def line_start(piece, ssem, rsem):
        @pl.when(z < PLANES - 1)
        def _():
            remote(piece(z), piece(z), ssem.at[0, z], rsem.at[z], up_dev).start()

        @pl.when(z > 0)
        def _():
            remote(piece(z), piece(z), ssem.at[1, z], rsem.at[z], down_dev).start()

    def order(j):
        flip = z >= PLANES // 2
        mine = jnp.where(flip, PLANES - 1 - z, z)
        s = 1 - mine if j == 0 else j + 1
        return jnp.where(flip, PLANES - 1 - s, s)

    def line_step(piece, ssem, rsem, j):
        s = order(j)
        arrived(piece(s), ssem.at[0, s], rsem.at[s])

        @pl.when(inner & (s < z))
        def _():
            remote(piece(s), piece(s), ssem.at[0, s], rsem.at[s], up_dev).start()

        @pl.when(inner & (s > z))
        def _():
            remote(piece(s), piece(s), ssem.at[1, s], rsem.at[s], down_dev).start()

        return s

    def line_end(piece, ssem, rsem):
        @pl.when(z < PLANES - 1)
        def _():
            remote(piece(z), piece(z), ssem.at[0, z], rsem.at[z], up_dev).wait_send()

        @pl.when(z > 0)
        def _():
            remote(piece(z), piece(z), ssem.at[1, z], rsem.at[z], down_dev).wait_send()

        for j in range(PLANES - 1):
            s = order(j)

            @pl.when(inner & (s < z))
            def _():
                remote(piece(s), piece(s), ssem.at[0, s], rsem.at[s], up_dev).wait_send()

            @pl.when(inner & (s > z))
            def _():
                remote(piece(s), piece(s), ssem.at[1, s], rsem.at[s], down_dev).wait_send()

    own_w1.wait()
    arrived(w1.at[at(ep + 1 - 2 * x, chunk), :], wx_ssem.at[0], wx_rsem.at[0])
    line_start(w1_at, w1_ssem, w1_rsem)

    arrived(n_at(c, 1 - x, y), n_ssem.at[0], n_rsem.at[0])
    send(n_at(c, 1 - x, y), n_at(c, 1 - x, y), n_ssem.at[3], n_rsem.at[3], y_dev)
    send(n_at(c, 1 - x, y), n_at(c, 1 - x, y), n_ssem.at[4], n_rsem.at[4], core_dev)
    for k in range(1, n_ep):
        arrived(x_part(c, y, peer(n_ep - k)), d_ssem.at[k], d_rsem.at[k])
    send(x_at(c, y), x_at(c, y), x_ssem.at[0], x_rsem.at[0], y_dev)
    send(x_at(c, y), x_at(c, y), x_ssem.at[1], x_rsem.at[1], core_dev)
    line_step(w1_at, w1_ssem, w1_rsem, 0)
    own_w2.wait()
    arrived(w2.at[z, :, at(1 - x, chunk)], wx_ssem.at[1], wx_rsem.at[1])
    line_start(w2_at, w2_ssem, w2_rsem)
    arrived(n_at(c, x, 1 - y), n_ssem.at[1], n_rsem.at[1])
    send(n_at(c, x, 1 - y), n_at(c, x, 1 - y), n_ssem.at[5], n_rsem.at[5], core_dev)
    arrived(x_at(c, 1 - y), x_ssem.at[0], x_rsem.at[0])
    send(x_at(c, 1 - y), x_at(c, 1 - y), x_ssem.at[2], x_rsem.at[2], core_dev)
    arrived(n_at(c, 1 - x, 1 - y), n_ssem.at[3], n_rsem.at[3])
    send(n_at(c, 1 - x, 1 - y), n_at(c, 1 - x, 1 - y), n_ssem.at[6], n_rsem.at[6], core_dev)
    line_step(w1_at, w1_ssem, w1_rsem, 1)

    arrived(x_at(1 - c, y), x_ssem.at[1], x_rsem.at[1])
    arrived(x_at(1 - c, 1 - y), x_ssem.at[2], x_rsem.at[2])
    load_in.wait()

    @pl.loop(0, ehid.shape[1] // 256)
    def _(i):
        ehid[:, at(i, 256)] = gelu(dot(xrows[...], ein[:, at(i, 256)])).astype(BF16)

    line_step(w1_at, w1_ssem, w1_rsem, 2)
    load_out.wait()

    @pl.loop(0, width // 256)
    def _(i):
        er_send[:, at(i, 256)] = dot(ehid[at(1 - c, 2 * rows), :], eout[:, at(i, 256)]).astype(BF16)
        er_keep[:, at(i, 256)] = dot(ehid[at(c, 2 * rows), :], eout[:, at(i, 256)])

    send(er_send, er_recv, e_ssem.at[0], e_rsem.at[0], core_dev)
    line_step(w2_at, w2_ssem, w2_rsem, 0)

    arrived(n_at(1 - c, x, y), n_ssem.at[2], n_rsem.at[2])
    arrived(n_at(1 - c, 1 - x, y), n_ssem.at[4], n_rsem.at[4])
    arrived(n_at(1 - c, x, 1 - y), n_ssem.at[5], n_rsem.at[5])
    arrived(n_at(1 - c, 1 - x, 1 - y), n_ssem.at[6], n_rsem.at[6])

    @pl.loop(0, normed.shape[0] // 256)
    def _(i):
        rhid[at(i, 256), :] = gelu(dot(normed[at(i, 256), :], w1[...])).astype(BF16)

    arrived(er_recv, e_ssem.at[0], e_rsem.at[0])
    ey_send[...] = (er_keep[at(1 - y, rows), :] + er_recv[at(1 - y, rows), :].astype(F32)).astype(BF16)
    send(ey_send, ey_recv, e_ssem.at[1], e_rsem.at[1], y_dev)
    ey_keep[...] = er_keep[at(y, rows), :] + er_recv[at(y, rows), :].astype(F32)

    def stage_a(s):
        pc_send[s] = dot(rhid[at(1 - c, 4 * rows), :], w2[s]).astype(BF16)
        send(pc_send.at[s], pc_recv.at[s], r_ssem.at[0, s], r_rsem.at[0, s], core_dev)
        pc_keep[s] = dot(rhid[at(c, 4 * rows), :], w2[s])

    def stage_b(s):
        arrived(pc_recv.at[s], r_ssem.at[0, s], r_rsem.at[0, s])
        away, stay = at(1 - x, 2 * rows), at(x, 2 * rows)
        px_send[s] = (pc_keep[s, away, :] + pc_recv[s, away, :].astype(F32)).astype(BF16)
        send(px_send.at[s], px_recv.at[s], r_ssem.at[1, s], r_rsem.at[1, s], x_dev)
        px_keep[s] = pc_keep[s, stay, :] + pc_recv[s, stay, :].astype(F32)

    def stage_c(s):
        arrived(px_recv.at[s], r_ssem.at[1, s], r_rsem.at[1, s])
        away, stay = at(1 - y, rows), at(y, rows)
        py_send[s] = (px_keep[s, away, :] + px_recv[s, away, :].astype(F32)).astype(BF16)
        send(py_send.at[s], py_recv.at[s], r_ssem.at[2, s], r_rsem.at[2, s], y_dev)
        py_keep[s] = px_keep[s, stay, :] + px_recv[s, stay, :].astype(F32)

    def stage_d(s):
        arrived(py_recv.at[s], r_ssem.at[2, s], r_rsem.at[2, s])
        res[s] = py_keep[s] + py_recv[s].astype(F32)

    s0, s1, s2, s3 = z, order(0), order(1), order(2)
    stage_a(s0)
    stage_a(s1)
    stage_b(s0)

    arrived(ey_recv, e_ssem.at[1], e_rsem.at[1])
    eb_send[...] = (ey_keep[...] + ey_recv[...].astype(F32)).astype(BF16)
    for k in range(1, n_ep):
        send(
            eb_send.at[at(peer(k), cap), :], back.at[at(ep, cap), :],
            b_ssem.at[k], b_rsem.at[k], dev(rep, peer(k)),
        )
    back[at(ep, cap), :] = eb_send[at(ep, cap), :]

    line_step(w2_at, w2_ssem, w2_rsem, 1)
    stage_a(s2)
    stage_b(s1)
    stage_c(s0)
    stage_b(s2)
    line_step(w2_at, w2_ssem, w2_rsem, 2)
    stage_a(s3)
    stage_c(s1)
    stage_d(s0)
    stage_b(s3)
    stage_c(s2)
    stage_d(s1)

    for k in range(1, n_ep):
        arrived(back.at[at(peer(n_ep - k), cap), :], b_ssem.at[k], b_rsem.at[k])
    same = lax.broadcasted_iota(jnp.int32, (rows, rows), 0) == lax.broadcasted_iota(
        jnp.int32, (rows, rows), 1
    )
    gate = jnp.sum(jnp.where(same, gates[...], 0.0), axis=1, keepdims=True)
    picked = lax.dot_general(
        table, back[...], (((0,), (0,)), ((), ())), preferred_element_type=F32
    )
    ey_keep[...] = tokens[...].astype(F32) + gate * picked

    stage_c(s3)
    stage_d(s2)
    stage_d(s3)
    for s in range(PLANES):
        columns = pl.ds(s * cols, cols)
        out[:, columns] = (ey_keep[:, columns] + res[s]).astype(BF16)

    for copy in sent:
        copy.wait_send()
    line_end(w1_at, w1_ssem, w1_rsem)
    line_end(w2_at, w2_ssem, w2_rsem)


def one_kernel(
    tokens, norm_gain, gates, expert_ids, slots, dropped, res_in, res_out, expert_in, expert_out
):
    rows, width = tokens.shape
    chunk = res_in.shape[0]
    half = res_in.shape[1] // 2
    cols = 2 * chunk
    units = expert_in.shape[2]
    vmem = pl.BlockSpec(memory_space=pltpu.VMEM)
    hbm = pl.BlockSpec(memory_space=pl.ANY)
    dma = pltpu.SemaphoreType.DMA
    scratch = [
        pltpu.VMEM((width, half), BF16),
        pltpu.VMEM((PLANES, half, cols), BF16),
        pltpu.VMEM((width, units), BF16),
        pltpu.VMEM((units, width), BF16),
        pltpu.VMEM((8 * rows, width), BF16),
        pltpu.VMEM((4 * rows, width), BF16),
        pltpu.VMEM((rows, width), BF16),
        pltpu.VMEM((4 * rows, units), BF16),
        pltpu.VMEM((2 * rows, width), BF16),
        pltpu.VMEM((2 * rows, width), F32),
        pltpu.VMEM((2 * rows, width), BF16),
        pltpu.VMEM((rows, width), BF16),
        pltpu.VMEM((rows, width), F32),
        pltpu.VMEM((rows, width), BF16),
        pltpu.VMEM((rows, width), BF16),
        pltpu.VMEM((rows, width), BF16),
        pltpu.VMEM((8 * rows, half), BF16),
    ]
    for part in (4, 2, 1):
        scratch += [
            pltpu.VMEM((PLANES, part * rows, cols), BF16),
            pltpu.VMEM((PLANES, part * rows, cols), F32),
            pltpu.VMEM((PLANES, part * rows, cols), BF16),
        ]
    scratch += [pltpu.VMEM((PLANES, rows, cols), F32)]
    scratch += [
        dma((4,)), dma((2,)), dma((2,)),
        dma((2, PLANES)), dma((PLANES,)), dma((2, PLANES)), dma((PLANES,)),
        dma((7,)), dma((7,)), dma((8,)), dma((8,)), dma((3,)), dma((3,)),
        dma((2,)), dma((2,)), dma((8,)), dma((8,)), dma((3, PLANES)), dma((3, PLANES)),
    ]
    return pl.pallas_call(
        layer_kernel,
        out_shape=jax.ShapeDtypeStruct((rows, width), BF16),
        in_specs=[vmem] * 6 + [hbm] * 4,
        out_specs=vmem,
        scratch_shapes=scratch,
        compiler_params=pltpu.CompilerParams(
            collective_id=0, has_side_effects=True, vmem_limit_bytes=60 * 1024 * 1024
        ),
    )(
        tokens, norm_gain.reshape(1, -1), gates.reshape(1, -1), expert_ids.reshape(1, -1),
        slots.reshape(1, -1), dropped.reshape(1, -1), res_in, res_out,
        expert_in.reshape(expert_in.shape[1:]), expert_out.reshape(expert_out.shape[1:]),
    )


def rms_norm(tokens, norm_gain):
    values = tokens.astype(jnp.float32)
    scale = lax.rsqrt(jnp.mean(values * values, axis=-1, keepdims=True) + 1e-06)
    return (values * scale * norm_gain).astype(jnp.bfloat16)


def on_device(
    tokens, norm_gain, gates, expert_ids, slots, dropped, res_in, res_out, expert_in, expert_out
):
    n_rep = lax.axis_size("rep")
    n_ep = lax.axis_size("ep")
    rows = tokens.shape[0]
    width = tokens.shape[1]
    cap = rows // n_ep
    normed = rms_norm(tokens, norm_gain)
    keep = 1 - dropped
    gathered, ids_all, slots_all, keep_all = (
        lax.all_gather(normed, "rep", axis=0, tiled=True),
        lax.all_gather(expert_ids, "rep", axis=0, tiled=True),
        lax.all_gather(slots, "rep", axis=0, tiled=True),
        lax.all_gather(keep, "rep", axis=0, tiled=True),
    )
    replica = jnp.arange(n_rep * rows, dtype=jnp.int32) // rows
    target = ids_all * (n_rep * cap) + replica * cap + slots_all
    places = jnp.arange(n_ep * n_rep * cap, dtype=jnp.int32)
    table = ((target[None, :] == places[:, None]) & (keep_all[None, :] == 1)).astype(jnp.bfloat16)
    buffer = (
        jnp.dot(table, gathered, preferred_element_type=jnp.float32)
        .astype(jnp.bfloat16)
        .reshape(n_ep, n_rep * cap, width)
    )
    block = lax.all_to_all(buffer, "ep", split_axis=0, concat_axis=0, tiled=True)
    flat = block.reshape(-1, width)
    hidden = jax.nn.gelu(
        jnp.dot(flat, expert_in[0], preferred_element_type=jnp.float32), approximate=True
    ).astype(jnp.bfloat16)
    result = jnp.dot(hidden, expert_out[0], preferred_element_type=jnp.float32)
    back = lax.all_to_all(
        result.reshape(block.shape[0], block.shape[1], width).astype(jnp.bfloat16),
        "ep",
        split_axis=0,
        concat_axis=0,
        tiled=True,
    ).astype(jnp.float32)
    picked = jnp.take(back.reshape(-1, width), jnp.where(keep_all == 1, target, 0), axis=0)
    partial_rows = jnp.where(keep_all[:, None] == 1, picked, 0.0)
    weight_in = lax.all_gather(res_in, "ep", axis=0, tiled=True)
    hidden = jax.nn.gelu(
        jnp.dot(gathered, weight_in, preferred_element_type=jnp.float32), approximate=True
    ).astype(jnp.bfloat16)
    weight_out = lax.all_gather(res_out, "ep", axis=1, tiled=True)
    res_branch = lax.psum_scatter(
        jnp.dot(hidden, weight_out, preferred_element_type=jnp.float32),
        "rep",
        scatter_dimension=0,
        tiled=True,
    )
    exp_branch = lax.psum_scatter(partial_rows, "rep", scatter_dimension=0, tiled=True)
    mixed = tokens.astype(jnp.float32) + res_branch + gates[:, None] * exp_branch
    return mixed.astype(jnp.bfloat16)


def solution(mesh):
    planes = mesh.shape["rep"] == 4 and mesh.shape["ep"] == 2 * PLANES
    return jax.shard_map(
        one_kernel if planes else on_device,
        mesh=mesh,
        in_specs=(
            P(("rep", "ep"), None),
            P(),
            P(("rep", "ep")),
            P(("rep", "ep")),
            P(("rep", "ep")),
            P(("rep", "ep")),
            P("ep", "rep"),
            P("rep", "ep"),
            P("ep", None, "rep"),
            P("ep", "rep", None),
        ),
        out_specs=P(("rep", "ep"), None),
        check_vma=False,
    )
```

```python
import jax
import jax.numpy as jnp
from jax import lax
from jax.experimental import pallas as pl
from jax.experimental.pallas import tpu as pltpu
from jax.sharding import PartitionSpec as P

F32 = jnp.float32
BF16 = jnp.bfloat16
PLANES = 4


def gelu(x):
    return x * (0.5 * (1.0 + jnp.tanh(0.7978845608028654 * (x + 0.044715 * (x * x * x)))))


def dot(a, b):
    return jnp.dot(a, b, preferred_element_type=F32)


def layer_kernel(
    tokens, gain, gates, ids, slots, dropped, res_in, res_out, exp_in, exp_out,
    out,
    w1, w2, ein, eout, normed, xrows, disp, ehid,
    er_send, er_keep, er_recv, ey_send, ey_keep, ey_recv, eb_send, back,
    rhid, pc_send, pc_keep, pc_recv, px_send, px_keep, px_recv, py_send, py_keep, py_recv,
    res,
    local_sem, wx_ssem, wx_rsem, w1_ssem, w1_rsem, w2_ssem, w2_rsem,
    n_ssem, n_rsem, d_ssem, d_rsem, x_ssem, x_rsem, e_ssem, e_rsem, b_ssem, b_rsem,
    r_ssem, r_rsem,
):
    rep, ep = lax.axis_index("rep"), lax.axis_index("ep")
    y, c = rep // 2, rep % 2
    z, x = ep // 2, ep % 2
    rows, width = tokens.shape
    n_ep = 2 * PLANES
    cap = rows // n_ep
    half = w1.shape[1]
    chunk = res_in.shape[0]
    cols = 2 * chunk

    def dev(r, e):
        return {"rep": r, "ep": e}

    core_dev = dev(rep + 1 - 2 * c, ep)
    y_dev = dev(rep + 2 - 4 * y, ep)
    x_dev = dev(rep, ep + 1 - 2 * x)
    up_dev, down_dev = dev(rep, ep + 2), dev(rep, ep - 2)

    def peer(k):
        return lax.rem(ep + k, n_ep)

    def remote(src, dst, ssem, rsem, device):
        return pltpu.make_async_remote_copy(
            src_ref=src, dst_ref=dst, send_sem=ssem, recv_sem=rsem,
            device_id=device, device_id_type=pl.DeviceIdType.MESH,
        )

    def arrived(dst, ssem, rsem):
        remote(dst, dst, ssem, rsem, core_dev).wait_recv()

    sent = []

    def send(src, dst, ssem, rsem, device):
        copy = remote(src, dst, ssem, rsem, device)
        copy.start()
        sent.append(copy)

    def at(i, n):
        return pl.ds(pl.multiple_of(i * n, n), n)

    barrier = pltpu.get_barrier_semaphore()
    for k in range(1, n_ep):
        pl.semaphore_signal(
            barrier, inc=1, device_id=dev(rep, peer(k)), device_id_type=pl.DeviceIdType.MESH
        )
    for device in (core_dev, y_dev):
        pl.semaphore_signal(barrier, inc=1, device_id=device, device_id_type=pl.DeviceIdType.MESH)

    own_w1 = pltpu.make_async_copy(res_in.at[:, at(x, half)], w1.at[at(ep, chunk), :], local_sem.at[0])
    own_w2 = pltpu.make_async_copy(
        res_out.at[at(x, half), :], w2.at[z, :, at(x, chunk)], local_sem.at[1]
    )
    load_in = pltpu.make_async_copy(exp_in, ein, local_sem.at[2])
    load_out = pltpu.make_async_copy(exp_out, eout, local_sem.at[3])
    for copy in (own_w1, own_w2, load_in, load_out):
        copy.start()

    pl.semaphore_wait(barrier, n_ep + 1)

    send(res_in.at[:, at(1 - x, half)], w1.at[at(ep, chunk), :], wx_ssem.at[0], wx_rsem.at[0], x_dev)

    values = tokens[...].astype(F32)
    scale = lax.rsqrt(jnp.mean(values * values, axis=-1, keepdims=True) + 1e-06)
    own_normed = (values * scale * gain[...]).astype(BF16)

    def n_at(cc, xx, yy):
        return normed.at[at(cc * 4 + xx * 2 + yy, rows), :]

    normed[at(c * 4 + x * 2 + y, rows), :] = own_normed

    target = ids[...] * cap + slots[...]
    places = lax.broadcasted_iota(jnp.int32, (n_ep * cap, rows), 0)
    table = jnp.where((places == target) & (dropped[...] == 0), 1.0, 0.0).astype(BF16)
    disp[...] = dot(table, own_normed).astype(BF16)

    def x_at(cc, yy):
        return xrows.at[at(cc * 2 + yy, rows), :]

    def x_part(cc, yy, e):
        return xrows.at[pl.ds(pl.multiple_of((cc * 2 + yy) * rows + e * cap, cap), cap), :]

    for k in range(1, n_ep):
        send(disp.at[at(peer(k), cap), :], x_part(c, y, ep), d_ssem.at[k], d_rsem.at[k], dev(rep, peer(k)))
    x_part(c, y, ep)[...] = disp[at(ep, cap), :]

    send(n_at(c, x, y), n_at(c, x, y), n_ssem.at[1], n_rsem.at[1], y_dev)
    send(n_at(c, x, y), n_at(c, x, y), n_ssem.at[2], n_rsem.at[2], core_dev)

    def w1_at(s):
        return w1.at[at(s, cols), :]

    def w2_at(s):
        return w2.at[s]

    inner = (z > 0) & (z < PLANES - 1)

    def line_start(piece, ssem, rsem):
        @pl.when(z < PLANES - 1)
        def _():
            remote(piece(z), piece(z), ssem.at[0, z], rsem.at[z], up_dev).start()

        @pl.when(z > 0)
        def _():
            remote(piece(z), piece(z), ssem.at[1, z], rsem.at[z], down_dev).start()

    def order(j):
        flip = z >= PLANES // 2
        mine = jnp.where(flip, PLANES - 1 - z, z)
        s = 1 - mine if j == 0 else j + 1
        return jnp.where(flip, PLANES - 1 - s, s)

    def line_wait(piece, ssem, rsem, j):
        s = order(j)

        @pl.when(jnp.logical_not(inner))
        def _():
            arrived(piece(s), ssem.at[0, s], rsem.at[s])

    def line_step(piece, ssem, rsem, j):
        s = order(j)

        @pl.when(inner)
        def _():
            arrived(piece(s), ssem.at[0, s], rsem.at[s])

        @pl.when(inner & (s < z))
        def _():
            remote(piece(s), piece(s), ssem.at[0, s], rsem.at[s], up_dev).start()

        @pl.when(inner & (s > z))
        def _():
            remote(piece(s), piece(s), ssem.at[1, s], rsem.at[s], down_dev).start()

    def line_end(piece, ssem, rsem):
        @pl.when(z < PLANES - 1)
        def _():
            remote(piece(z), piece(z), ssem.at[0, z], rsem.at[z], up_dev).wait_send()

        @pl.when(z > 0)
        def _():
            remote(piece(z), piece(z), ssem.at[1, z], rsem.at[z], down_dev).wait_send()

        for j in range(PLANES - 1):
            s = order(j)

            @pl.when(inner & (s < z))
            def _():
                remote(piece(s), piece(s), ssem.at[0, s], rsem.at[s], up_dev).wait_send()

            @pl.when(inner & (s > z))
            def _():
                remote(piece(s), piece(s), ssem.at[1, s], rsem.at[s], down_dev).wait_send()

    own_w1.wait()
    arrived(w1.at[at(ep + 1 - 2 * x, chunk), :], wx_ssem.at[0], wx_rsem.at[0])
    line_start(w1_at, w1_ssem, w1_rsem)

    send(n_at(c, x, y), n_at(c, x, y), n_ssem.at[0], n_rsem.at[0], x_dev)
    send(
        res_out.at[at(1 - x, half), :], w2.at[z, :, at(x, chunk)],
        wx_ssem.at[1], wx_rsem.at[1], x_dev,
    )
    for k in range(1, n_ep):
        arrived(x_part(c, y, peer(n_ep - k)), d_ssem.at[k], d_rsem.at[k])
    send(x_at(c, y), x_at(c, y), x_ssem.at[0], x_rsem.at[0], y_dev)
    send(x_at(c, y), x_at(c, y), x_ssem.at[1], x_rsem.at[1], core_dev)
    arrived(n_at(c, x, 1 - y), n_ssem.at[1], n_rsem.at[1])
    send(n_at(c, x, 1 - y), n_at(c, x, 1 - y), n_ssem.at[5], n_rsem.at[5], core_dev)
    line_step(w1_at, w1_ssem, w1_rsem, 0)
    line_step(w1_at, w1_ssem, w1_rsem, 1)
    arrived(n_at(c, 1 - x, y), n_ssem.at[0], n_rsem.at[0])
    send(n_at(c, 1 - x, y), n_at(c, 1 - x, y), n_ssem.at[3], n_rsem.at[3], y_dev)
    send(n_at(c, 1 - x, y), n_at(c, 1 - x, y), n_ssem.at[4], n_rsem.at[4], core_dev)
    own_w2.wait()
    arrived(w2.at[z, :, at(1 - x, chunk)], wx_ssem.at[1], wx_rsem.at[1])
    line_start(w2_at, w2_ssem, w2_rsem)
    arrived(x_at(c, 1 - y), x_ssem.at[0], x_rsem.at[0])
    send(x_at(c, 1 - y), x_at(c, 1 - y), x_ssem.at[2], x_rsem.at[2], core_dev)
    line_step(w1_at, w1_ssem, w1_rsem, 2)

    arrived(x_at(1 - c, y), x_ssem.at[1], x_rsem.at[1])
    arrived(x_at(1 - c, 1 - y), x_ssem.at[2], x_rsem.at[2])
    load_in.wait()

    @pl.loop(0, ehid.shape[1] // 256)
    def _(i):
        ehid[:, at(i, 256)] = gelu(dot(xrows[...], ein[:, at(i, 256)])).astype(BF16)

    load_out.wait()

    @pl.loop(0, width // 256)
    def _(i):
        er_send[:, at(i, 256)] = dot(ehid[at(1 - c, 2 * rows), :], eout[:, at(i, 256)]).astype(BF16)
        er_keep[:, at(i, 256)] = dot(ehid[at(c, 2 * rows), :], eout[:, at(i, 256)])

    send(er_send, er_recv, e_ssem.at[0], e_rsem.at[0], core_dev)
    arrived(er_recv, e_ssem.at[0], e_rsem.at[0])
    ey_send[...] = (er_keep[at(1 - y, rows), :] + er_recv[at(1 - y, rows), :].astype(F32)).astype(BF16)
    send(ey_send, ey_recv, e_ssem.at[1], e_rsem.at[1], y_dev)
    ey_keep[...] = er_keep[at(y, rows), :] + er_recv[at(y, rows), :].astype(F32)

    arrived(n_at(c, 1 - x, 1 - y), n_ssem.at[3], n_rsem.at[3])
    send(n_at(c, 1 - x, 1 - y), n_at(c, 1 - x, 1 - y), n_ssem.at[6], n_rsem.at[6], core_dev)
    arrived(n_at(1 - c, x, y), n_ssem.at[2], n_rsem.at[2])
    arrived(n_at(1 - c, 1 - x, y), n_ssem.at[4], n_rsem.at[4])
    arrived(n_at(1 - c, x, 1 - y), n_ssem.at[5], n_rsem.at[5])
    arrived(n_at(1 - c, 1 - x, 1 - y), n_ssem.at[6], n_rsem.at[6])

    for j in range(PLANES - 1):
        line_wait(w1_at, w1_ssem, w1_rsem, j)

    @pl.loop(0, normed.shape[0] // 256)
    def _(i):
        rhid[at(i, 256), :] = gelu(dot(normed[at(i, 256), :], w1[...])).astype(BF16)

    def stage_a(s):
        pc_send[s] = dot(rhid[at(1 - c, 4 * rows), :], w2[s]).astype(BF16)
        send(pc_send.at[s], pc_recv.at[s], r_ssem.at[0, s], r_rsem.at[0, s], core_dev)
        pc_keep[s] = dot(rhid[at(c, 4 * rows), :], w2[s])

    def stage_b(s):
        arrived(pc_recv.at[s], r_ssem.at[0, s], r_rsem.at[0, s])
        away, stay = at(1 - x, 2 * rows), at(x, 2 * rows)
        px_send[s] = (pc_keep[s, away, :] + pc_recv[s, away, :].astype(F32)).astype(BF16)
        send(px_send.at[s], px_recv.at[s], r_ssem.at[1, s], r_rsem.at[1, s], x_dev)
        px_keep[s] = pc_keep[s, stay, :] + pc_recv[s, stay, :].astype(F32)

    def stage_c(s):
        arrived(px_recv.at[s], r_ssem.at[1, s], r_rsem.at[1, s])
        away, stay = at(1 - y, rows), at(y, rows)
        py_send[s] = (px_keep[s, away, :] + px_recv[s, away, :].astype(F32)).astype(BF16)
        send(py_send.at[s], py_recv.at[s], r_ssem.at[2, s], r_rsem.at[2, s], y_dev)
        py_keep[s] = px_keep[s, stay, :] + px_recv[s, stay, :].astype(F32)

    def stage_d(s):
        arrived(py_recv.at[s], r_ssem.at[2, s], r_rsem.at[2, s])
        res[s] = py_keep[s] + py_recv[s].astype(F32)

    s0, s1, s2, s3 = z, order(0), order(1), order(2)
    line_step(w2_at, w2_ssem, w2_rsem, 0)
    line_step(w2_at, w2_ssem, w2_rsem, 1)
    stage_a(s0)
    arrived(ey_recv, e_ssem.at[1], e_rsem.at[1])
    eb_send[...] = (ey_keep[...] + ey_recv[...].astype(F32)).astype(BF16)
    for k in range(1, n_ep):
        send(
            eb_send.at[at(peer(k), cap), :], back.at[at(ep, cap), :],
            b_ssem.at[k], b_rsem.at[k], dev(rep, peer(k)),
        )
    back[at(ep, cap), :] = eb_send[at(ep, cap), :]

    stage_b(s0)
    line_wait(w2_at, w2_ssem, w2_rsem, 0)
    stage_a(s1)
    stage_b(s1)
    line_step(w2_at, w2_ssem, w2_rsem, 2)
    stage_c(s0)
    line_wait(w2_at, w2_ssem, w2_rsem, 1)
    stage_a(s2)
    stage_b(s2)
    stage_c(s1)
    stage_d(s0)
    for k in range(1, n_ep):
        arrived(back.at[at(peer(n_ep - k), cap), :], b_ssem.at[k], b_rsem.at[k])
    same = lax.broadcasted_iota(jnp.int32, (rows, rows), 0) == lax.broadcasted_iota(
        jnp.int32, (rows, rows), 1
    )
    gate = jnp.sum(jnp.where(same, gates[...], 0.0), axis=1, keepdims=True)
    picked = lax.dot_general(
        table, back[...], (((0,), (0,)), ((), ())), preferred_element_type=F32
    )
    ey_keep[...] = tokens[...].astype(F32) + gate * picked

    stage_c(s2)
    stage_d(s1)
    line_wait(w2_at, w2_ssem, w2_rsem, 2)
    stage_a(s3)
    stage_b(s3)
    stage_d(s2)
    stage_c(s3)
    stage_d(s3)
    for s in range(PLANES):
        columns = pl.ds(s * cols, cols)
        out[:, columns] = (ey_keep[:, columns] + res[s]).astype(BF16)

    for copy in sent:
        copy.wait_send()
    line_end(w1_at, w1_ssem, w1_rsem)
    line_end(w2_at, w2_ssem, w2_rsem)


def one_kernel(
    tokens, norm_gain, gates, expert_ids, slots, dropped, res_in, res_out, expert_in, expert_out
):
    rows, width = tokens.shape
    chunk = res_in.shape[0]
    half = res_in.shape[1] // 2
    cols = 2 * chunk
    units = expert_in.shape[2]
    vmem = pl.BlockSpec(memory_space=pltpu.VMEM)
    hbm = pl.BlockSpec(memory_space=pl.ANY)
    dma = pltpu.SemaphoreType.DMA
    scratch = [
        pltpu.VMEM((width, half), BF16),
        pltpu.VMEM((PLANES, half, cols), BF16),
        pltpu.VMEM((width, units), BF16),
        pltpu.VMEM((units, width), BF16),
        pltpu.VMEM((8 * rows, width), BF16),
        pltpu.VMEM((4 * rows, width), BF16),
        pltpu.VMEM((rows, width), BF16),
        pltpu.VMEM((4 * rows, units), BF16),
        pltpu.VMEM((2 * rows, width), BF16),
        pltpu.VMEM((2 * rows, width), F32),
        pltpu.VMEM((2 * rows, width), BF16),
        pltpu.VMEM((rows, width), BF16),
        pltpu.VMEM((rows, width), F32),
        pltpu.VMEM((rows, width), BF16),
        pltpu.VMEM((rows, width), BF16),
        pltpu.VMEM((rows, width), BF16),
        pltpu.VMEM((8 * rows, half), BF16),
    ]
    for part in (4, 2, 1):
        scratch += [
            pltpu.VMEM((PLANES, part * rows, cols), BF16),
            pltpu.VMEM((PLANES, part * rows, cols), F32),
            pltpu.VMEM((PLANES, part * rows, cols), BF16),
        ]
    scratch += [pltpu.VMEM((PLANES, rows, cols), F32)]
    scratch += [
        dma((4,)), dma((2,)), dma((2,)),
        dma((2, PLANES)), dma((PLANES,)), dma((2, PLANES)), dma((PLANES,)),
        dma((7,)), dma((7,)), dma((8,)), dma((8,)), dma((3,)), dma((3,)),
        dma((2,)), dma((2,)), dma((8,)), dma((8,)), dma((3, PLANES)), dma((3, PLANES)),
    ]
    return pl.pallas_call(
        layer_kernel,
        out_shape=jax.ShapeDtypeStruct((rows, width), BF16),
        in_specs=[vmem] * 6 + [hbm] * 4,
        out_specs=vmem,
        scratch_shapes=scratch,
        compiler_params=pltpu.CompilerParams(
            collective_id=0, has_side_effects=True, vmem_limit_bytes=60 * 1024 * 1024
        ),
    )(
        tokens, norm_gain.reshape(1, -1), gates.reshape(1, -1), expert_ids.reshape(1, -1),
        slots.reshape(1, -1), dropped.reshape(1, -1), res_in, res_out,
        expert_in.reshape(expert_in.shape[1:]), expert_out.reshape(expert_out.shape[1:]),
    )


def rms_norm(tokens, norm_gain):
    values = tokens.astype(jnp.float32)
    scale = lax.rsqrt(jnp.mean(values * values, axis=-1, keepdims=True) + 1e-06)
    return (values * scale * norm_gain).astype(jnp.bfloat16)


def on_device(
    tokens, norm_gain, gates, expert_ids, slots, dropped, res_in, res_out, expert_in, expert_out
):
    n_rep = lax.axis_size("rep")
    n_ep = lax.axis_size("ep")
    rows = tokens.shape[0]
    width = tokens.shape[1]
    cap = rows // n_ep
    normed = rms_norm(tokens, norm_gain)
    keep = 1 - dropped
    gathered, ids_all, slots_all, keep_all = (
        lax.all_gather(normed, "rep", axis=0, tiled=True),
        lax.all_gather(expert_ids, "rep", axis=0, tiled=True),
        lax.all_gather(slots, "rep", axis=0, tiled=True),
        lax.all_gather(keep, "rep", axis=0, tiled=True),
    )
    replica = jnp.arange(n_rep * rows, dtype=jnp.int32) // rows
    target = ids_all * (n_rep * cap) + replica * cap + slots_all
    places = jnp.arange(n_ep * n_rep * cap, dtype=jnp.int32)
    table = ((target[None, :] == places[:, None]) & (keep_all[None, :] == 1)).astype(jnp.bfloat16)
    buffer = (
        jnp.dot(table, gathered, preferred_element_type=jnp.float32)
        .astype(jnp.bfloat16)
        .reshape(n_ep, n_rep * cap, width)
    )
    block = lax.all_to_all(buffer, "ep", split_axis=0, concat_axis=0, tiled=True)
    flat = block.reshape(-1, width)
    hidden = jax.nn.gelu(
        jnp.dot(flat, expert_in[0], preferred_element_type=jnp.float32), approximate=True
    ).astype(jnp.bfloat16)
    result = jnp.dot(hidden, expert_out[0], preferred_element_type=jnp.float32)
    back = lax.all_to_all(
        result.reshape(block.shape[0], block.shape[1], width).astype(jnp.bfloat16),
        "ep",
        split_axis=0,
        concat_axis=0,
        tiled=True,
    ).astype(jnp.float32)
    picked = jnp.take(back.reshape(-1, width), jnp.where(keep_all == 1, target, 0), axis=0)
    partial_rows = jnp.where(keep_all[:, None] == 1, picked, 0.0)
    weight_in = lax.all_gather(res_in, "ep", axis=0, tiled=True)
    hidden = jax.nn.gelu(
        jnp.dot(gathered, weight_in, preferred_element_type=jnp.float32), approximate=True
    ).astype(jnp.bfloat16)
    weight_out = lax.all_gather(res_out, "ep", axis=1, tiled=True)
    res_branch = lax.psum_scatter(
        jnp.dot(hidden, weight_out, preferred_element_type=jnp.float32),
        "rep",
        scatter_dimension=0,
        tiled=True,
    )
    exp_branch = lax.psum_scatter(partial_rows, "rep", scatter_dimension=0, tiled=True)
    mixed = tokens.astype(jnp.float32) + res_branch + gates[:, None] * exp_branch
    return mixed.astype(jnp.bfloat16)


def solution(mesh):
    planes = mesh.shape["rep"] == 4 and mesh.shape["ep"] == 2 * PLANES
    return jax.shard_map(
        one_kernel if planes else on_device,
        mesh=mesh,
        in_specs=(
            P(("rep", "ep"), None),
            P(),
            P(("rep", "ep")),
            P(("rep", "ep")),
            P(("rep", "ep")),
            P(("rep", "ep")),
            P("ep", "rep"),
            P("rep", "ep"),
            P("ep", None, "rep"),
            P("ep", "rep", None),
        ),
        out_specs=P(("rep", "ep"), None),
        check_vma=False,
    )
```

```python
import jax
import jax.numpy as jnp
from jax import lax
from jax.experimental import pallas as pl
from jax.experimental.pallas import tpu as pltpu
from jax.sharding import PartitionSpec as P

F32 = jnp.float32
BF16 = jnp.bfloat16
PLANES = 4


def gelu(x):
    return x * (0.5 * (1.0 + jnp.tanh(0.7978845608028654 * (x + 0.044715 * (x * x * x)))))


def dot(a, b):
    return jnp.dot(a, b, preferred_element_type=F32)


def layer_kernel(
    tokens, gain, gates, ids, slots, dropped, res_in, res_out, exp_in, exp_out,
    out,
    w1, w2, ein, eout, normed, xrows, disp, ehid,
    er_send, er_keep, er_recv, ey_send, ey_keep, ey_recv, eb_send, back,
    rhid, pc_send, pc_keep, pc_recv, px_send, px_keep, px_recv, py_send, py_keep, py_recv,
    res,
    local_sem, wx_ssem, wx_rsem, w1_ssem, w1_rsem, w2_ssem, w2_rsem,
    n_ssem, n_rsem, d_ssem, d_rsem, x_ssem, x_rsem, e_ssem, e_rsem, b_ssem, b_rsem,
    r_ssem, r_rsem,
):
    rep, ep = lax.axis_index("rep"), lax.axis_index("ep")
    y, c = rep // 2, rep % 2
    z, x = ep // 2, ep % 2
    rows, width = tokens.shape
    n_ep = 2 * PLANES
    cap = rows // n_ep
    half = w1.shape[1]
    chunk = res_in.shape[0]
    cols = 2 * chunk

    def dev(r, e):
        return {"rep": r, "ep": e}

    core_dev = dev(rep + 1 - 2 * c, ep)
    y_dev = dev(rep + 2 - 4 * y, ep)
    x_dev = dev(rep, ep + 1 - 2 * x)
    up_dev, down_dev = dev(rep, ep + 2), dev(rep, ep - 2)

    def peer(k):
        return lax.rem(ep + k, n_ep)

    def remote(src, dst, ssem, rsem, device):
        return pltpu.make_async_remote_copy(
            src_ref=src, dst_ref=dst, send_sem=ssem, recv_sem=rsem,
            device_id=device, device_id_type=pl.DeviceIdType.MESH,
        )

    def arrived(dst, ssem, rsem):
        remote(dst, dst, ssem, rsem, core_dev).wait_recv()

    sent = []

    def send(src, dst, ssem, rsem, device):
        copy = remote(src, dst, ssem, rsem, device)
        copy.start()
        sent.append(copy)

    def at(i, n):
        return pl.ds(pl.multiple_of(i * n, n), n)

    barrier = pltpu.get_barrier_semaphore()
    for k in range(1, n_ep):
        pl.semaphore_signal(
            barrier, inc=1, device_id=dev(rep, peer(k)), device_id_type=pl.DeviceIdType.MESH
        )
    for device in (core_dev, y_dev):
        pl.semaphore_signal(barrier, inc=1, device_id=device, device_id_type=pl.DeviceIdType.MESH)

    own_w1 = pltpu.make_async_copy(res_in.at[:, at(x, half)], w1.at[at(ep, chunk), :], local_sem.at[0])
    own_w2 = pltpu.make_async_copy(
        res_out.at[at(x, half), :], w2.at[z, :, at(x, chunk)], local_sem.at[1]
    )
    load_in = pltpu.make_async_copy(exp_in, ein, local_sem.at[2])
    load_out = pltpu.make_async_copy(exp_out, eout, local_sem.at[3])
    for copy in (own_w1, own_w2, load_in, load_out):
        copy.start()

    pl.semaphore_wait(barrier, n_ep + 1)

    send(res_in.at[:, at(1 - x, half)], w1.at[at(ep, chunk), :], wx_ssem.at[0], wx_rsem.at[0], x_dev)

    def w1_at(s, h):
        return w1.at[at(2 * s + h, chunk), :]

    def w2_at(s, h):
        return w2.at[s, :, at(h, chunk)]

    inner = (z > 0) & (z < PLANES - 1)

    def line_copy(piece, ssem, rsem, s, h, way):
        device = down_dev if way else up_dev
        return remote(piece(s, h), piece(s, h), ssem.at[way, h, s], rsem.at[h, s], device)

    def line_start(piece, ssem, rsem, h):
        @pl.when(z < PLANES - 1)
        def _():
            line_copy(piece, ssem, rsem, z, h, 0).start()

        @pl.when(z > 0)
        def _():
            line_copy(piece, ssem, rsem, z, h, 1).start()

    def order(j):
        flip = z >= PLANES // 2
        mine = jnp.where(flip, PLANES - 1 - z, z)
        s = 1 - mine if j == 0 else j + 1
        return jnp.where(flip, PLANES - 1 - s, s)

    def line_wait(piece, ssem, rsem, j, halves=(0, 1)):
        s = order(j)

        @pl.when(jnp.logical_not(inner))
        def _():
            for h in halves:
                line_copy(piece, ssem, rsem, s, h, 0).wait_recv()

    def line_step(piece, ssem, rsem, j):
        s = order(j)
        for h in (0, 1):
            @pl.when(inner)
            def _():
                line_copy(piece, ssem, rsem, s, h, 0).wait_recv()

            @pl.when(inner & (s < z))
            def _():
                line_copy(piece, ssem, rsem, s, h, 0).start()

            @pl.when(inner & (s > z))
            def _():
                line_copy(piece, ssem, rsem, s, h, 1).start()

    def line_end(piece, ssem, rsem):
        for h in (0, 1):
            @pl.when(z < PLANES - 1)
            def _():
                line_copy(piece, ssem, rsem, z, h, 0).wait_send()

            @pl.when(z > 0)
            def _():
                line_copy(piece, ssem, rsem, z, h, 1).wait_send()

            for j in range(PLANES - 1):
                s = order(j)

                @pl.when(inner & (s < z))
                def _():
                    line_copy(piece, ssem, rsem, s, h, 0).wait_send()

                @pl.when(inner & (s > z))
                def _():
                    line_copy(piece, ssem, rsem, s, h, 1).wait_send()

    own_w1.wait()
    line_start(w1_at, w1_ssem, w1_rsem, x)

    values = tokens[...].astype(F32)
    scale = lax.rsqrt(jnp.mean(values * values, axis=-1, keepdims=True) + 1e-06)
    own_normed = (values * scale * gain[...]).astype(BF16)

    def n_at(cc, xx, yy):
        return normed.at[at(cc * 4 + xx * 2 + yy, rows), :]

    normed[at(c * 4 + x * 2 + y, rows), :] = own_normed

    target = ids[...] * cap + slots[...]
    places = lax.broadcasted_iota(jnp.int32, (n_ep * cap, rows), 0)
    table = jnp.where((places == target) & (dropped[...] == 0), 1.0, 0.0).astype(BF16)
    disp[...] = dot(table, own_normed).astype(BF16)

    def x_at(cc, yy):
        return xrows.at[at(cc * 2 + yy, rows), :]

    def x_part(cc, yy, e):
        return xrows.at[pl.ds(pl.multiple_of((cc * 2 + yy) * rows + e * cap, cap), cap), :]

    for k in range(1, n_ep):
        send(disp.at[at(peer(k), cap), :], x_part(c, y, ep), d_ssem.at[k], d_rsem.at[k], dev(rep, peer(k)))
    x_part(c, y, ep)[...] = disp[at(ep, cap), :]

    send(n_at(c, x, y), n_at(c, x, y), n_ssem.at[1], n_rsem.at[1], y_dev)
    send(n_at(c, x, y), n_at(c, x, y), n_ssem.at[2], n_rsem.at[2], core_dev)

    arrived(w1.at[at(ep + 1 - 2 * x, chunk), :], wx_ssem.at[0], wx_rsem.at[0])
    line_start(w1_at, w1_ssem, w1_rsem, 1 - x)

    send(n_at(c, x, y), n_at(c, x, y), n_ssem.at[0], n_rsem.at[0], x_dev)
    send(
        res_out.at[at(1 - x, half), :], w2.at[z, :, at(x, chunk)],
        wx_ssem.at[1], wx_rsem.at[1], x_dev,
    )
    for k in range(1, n_ep):
        arrived(x_part(c, y, peer(n_ep - k)), d_ssem.at[k], d_rsem.at[k])
    send(x_at(c, y), x_at(c, y), x_ssem.at[0], x_rsem.at[0], y_dev)
    send(x_at(c, y), x_at(c, y), x_ssem.at[1], x_rsem.at[1], core_dev)
    arrived(n_at(c, x, 1 - y), n_ssem.at[1], n_rsem.at[1])
    send(n_at(c, x, 1 - y), n_at(c, x, 1 - y), n_ssem.at[5], n_rsem.at[5], core_dev)
    line_step(w1_at, w1_ssem, w1_rsem, 0)
    line_step(w1_at, w1_ssem, w1_rsem, 1)
    arrived(n_at(c, 1 - x, y), n_ssem.at[0], n_rsem.at[0])
    send(n_at(c, 1 - x, y), n_at(c, 1 - x, y), n_ssem.at[3], n_rsem.at[3], y_dev)
    send(n_at(c, 1 - x, y), n_at(c, 1 - x, y), n_ssem.at[4], n_rsem.at[4], core_dev)
    own_w2.wait()
    arrived(w2.at[z, :, at(1 - x, chunk)], wx_ssem.at[1], wx_rsem.at[1])
    line_start(w2_at, w2_ssem, w2_rsem, 0)
    line_start(w2_at, w2_ssem, w2_rsem, 1)
    arrived(x_at(c, 1 - y), x_ssem.at[0], x_rsem.at[0])
    send(x_at(c, 1 - y), x_at(c, 1 - y), x_ssem.at[2], x_rsem.at[2], core_dev)
    line_step(w1_at, w1_ssem, w1_rsem, 2)

    arrived(x_at(1 - c, y), x_ssem.at[1], x_rsem.at[1])
    arrived(x_at(1 - c, 1 - y), x_ssem.at[2], x_rsem.at[2])
    load_in.wait()

    @pl.loop(0, ehid.shape[1] // 256)
    def _(i):
        ehid[:, at(i, 256)] = gelu(dot(xrows[...], ein[:, at(i, 256)])).astype(BF16)

    load_out.wait()

    @pl.loop(0, width // 256)
    def _(i):
        er_send[:, at(i, 256)] = dot(ehid[at(1 - c, 2 * rows), :], eout[:, at(i, 256)]).astype(BF16)
        er_keep[:, at(i, 256)] = dot(ehid[at(c, 2 * rows), :], eout[:, at(i, 256)])

    send(er_send, er_recv, e_ssem.at[0], e_rsem.at[0], core_dev)
    arrived(er_recv, e_ssem.at[0], e_rsem.at[0])
    ey_send[...] = (er_keep[at(1 - y, rows), :] + er_recv[at(1 - y, rows), :].astype(F32)).astype(BF16)
    send(ey_send, ey_recv, e_ssem.at[1], e_rsem.at[1], y_dev)
    ey_keep[...] = er_keep[at(y, rows), :] + er_recv[at(y, rows), :].astype(F32)

    arrived(n_at(c, 1 - x, 1 - y), n_ssem.at[3], n_rsem.at[3])
    send(n_at(c, 1 - x, 1 - y), n_at(c, 1 - x, 1 - y), n_ssem.at[6], n_rsem.at[6], core_dev)
    arrived(n_at(1 - c, x, y), n_ssem.at[2], n_rsem.at[2])
    arrived(n_at(1 - c, 1 - x, y), n_ssem.at[4], n_rsem.at[4])
    arrived(n_at(1 - c, x, 1 - y), n_ssem.at[5], n_rsem.at[5])
    arrived(n_at(1 - c, 1 - x, 1 - y), n_ssem.at[6], n_rsem.at[6])

    for j in range(PLANES - 1):
        line_wait(w1_at, w1_ssem, w1_rsem, j)

    @pl.loop(0, normed.shape[0] // 256)
    def _(i):
        rhid[at(i, 256), :] = gelu(dot(normed[at(i, 256), :], w1[...])).astype(BF16)

    def stage_a(s, q, cs):
        pc_send[s, :, cs] = dot(rhid[at(1 - c, 4 * rows), :], w2[s, :, cs]).astype(BF16)
        send(pc_send.at[s, :, cs], pc_recv.at[s, :, cs], r_ssem.at[0, q], r_rsem.at[0, q], core_dev)
        pc_keep[s, :, cs] = dot(rhid[at(c, 4 * rows), :], w2[s, :, cs])

    def stage_b(s, q, cs):
        arrived(pc_recv.at[s, :, cs], r_ssem.at[0, q], r_rsem.at[0, q])
        away, stay = at(1 - x, 2 * rows), at(x, 2 * rows)
        px_send[s, :, cs] = (pc_keep[s, away, cs] + pc_recv[s, away, cs].astype(F32)).astype(BF16)
        send(px_send.at[s, :, cs], px_recv.at[s, :, cs], r_ssem.at[1, q], r_rsem.at[1, q], x_dev)
        px_keep[s, :, cs] = pc_keep[s, stay, cs] + pc_recv[s, stay, cs].astype(F32)

    def stage_c(s, q, cs):
        arrived(px_recv.at[s, :, cs], r_ssem.at[1, q], r_rsem.at[1, q])
        away, stay = at(1 - y, rows), at(y, rows)
        py_send[s, :, cs] = (px_keep[s, away, cs] + px_recv[s, away, cs].astype(F32)).astype(BF16)
        send(py_send.at[s, :, cs], py_recv.at[s, :, cs], r_ssem.at[2, q], r_rsem.at[2, q], y_dev)
        py_keep[s, :, cs] = px_keep[s, stay, cs] + px_recv[s, stay, cs].astype(F32)

    def stage_d(s, q, cs):
        arrived(py_recv.at[s, :, cs], r_ssem.at[2, q], r_rsem.at[2, q])
        res[s, :, cs] = py_keep[s, :, cs] + py_recv[s, :, cs].astype(F32)

    s0, s1, s2, s3 = z, order(0), order(1), order(2)
    whole, left, right = pl.ds(0, cols), pl.ds(0, chunk), pl.ds(chunk, chunk)
    line_step(w2_at, w2_ssem, w2_rsem, 0)
    line_step(w2_at, w2_ssem, w2_rsem, 1)
    stage_a(s0, s0, whole)
    arrived(ey_recv, e_ssem.at[1], e_rsem.at[1])
    eb_send[...] = (ey_keep[...] + ey_recv[...].astype(F32)).astype(BF16)
    for k in range(1, n_ep):
        send(
            eb_send.at[at(peer(k), cap), :], back.at[at(ep, cap), :],
            b_ssem.at[k], b_rsem.at[k], dev(rep, peer(k)),
        )
    back[at(ep, cap), :] = eb_send[at(ep, cap), :]

    stage_b(s0, s0, whole)
    line_wait(w2_at, w2_ssem, w2_rsem, 0)
    stage_a(s1, s1, whole)
    stage_b(s1, s1, whole)
    line_step(w2_at, w2_ssem, w2_rsem, 2)
    stage_c(s0, s0, whole)
    line_wait(w2_at, w2_ssem, w2_rsem, 1)
    stage_a(s2, s2, whole)
    stage_b(s2, s2, whole)
    stage_c(s1, s1, whole)
    stage_d(s0, s0, whole)
    for k in range(1, n_ep):
        arrived(back.at[at(peer(n_ep - k), cap), :], b_ssem.at[k], b_rsem.at[k])
    same = lax.broadcasted_iota(jnp.int32, (rows, rows), 0) == lax.broadcasted_iota(
        jnp.int32, (rows, rows), 1
    )
    gate = jnp.sum(jnp.where(same, gates[...], 0.0), axis=1, keepdims=True)
    picked = lax.dot_general(
        table, back[...], (((0,), (0,)), ((), ())), preferred_element_type=F32
    )
    ey_keep[...] = tokens[...].astype(F32) + gate * picked

    stage_c(s2, s2, whole)
    stage_d(s1, s1, whole)
    line_wait(w2_at, w2_ssem, w2_rsem, 2, (0,))
    stage_a(s3, s3, left)
    stage_d(s2, s2, whole)
    stage_b(s3, s3, left)
    line_wait(w2_at, w2_ssem, w2_rsem, 2, (1,))
    stage_a(s3, PLANES, right)
    stage_b(s3, PLANES, right)
    stage_c(s3, s3, left)
    stage_c(s3, PLANES, right)
    stage_d(s3, s3, left)
    stage_d(s3, PLANES, right)
    for s in range(PLANES):
        columns = pl.ds(s * cols, cols)
        out[:, columns] = (ey_keep[:, columns] + res[s]).astype(BF16)

    for copy in sent:
        copy.wait_send()
    line_end(w1_at, w1_ssem, w1_rsem)
    line_end(w2_at, w2_ssem, w2_rsem)


def one_kernel(
    tokens, norm_gain, gates, expert_ids, slots, dropped, res_in, res_out, expert_in, expert_out
):
    rows, width = tokens.shape
    chunk = res_in.shape[0]
    half = res_in.shape[1] // 2
    cols = 2 * chunk
    units = expert_in.shape[2]
    vmem = pl.BlockSpec(memory_space=pltpu.VMEM)
    hbm = pl.BlockSpec(memory_space=pl.ANY)
    dma = pltpu.SemaphoreType.DMA
    scratch = [
        pltpu.VMEM((width, half), BF16),
        pltpu.VMEM((PLANES, half, cols), BF16),
        pltpu.VMEM((width, units), BF16),
        pltpu.VMEM((units, width), BF16),
        pltpu.VMEM((8 * rows, width), BF16),
        pltpu.VMEM((4 * rows, width), BF16),
        pltpu.VMEM((rows, width), BF16),
        pltpu.VMEM((4 * rows, units), BF16),
        pltpu.VMEM((2 * rows, width), BF16),
        pltpu.VMEM((2 * rows, width), F32),
        pltpu.VMEM((2 * rows, width), BF16),
        pltpu.VMEM((rows, width), BF16),
        pltpu.VMEM((rows, width), F32),
        pltpu.VMEM((rows, width), BF16),
        pltpu.VMEM((rows, width), BF16),
        pltpu.VMEM((rows, width), BF16),
        pltpu.VMEM((8 * rows, half), BF16),
    ]
    for part in (4, 2, 1):
        scratch += [
            pltpu.VMEM((PLANES, part * rows, cols), BF16),
            pltpu.VMEM((PLANES, part * rows, cols), F32),
            pltpu.VMEM((PLANES, part * rows, cols), BF16),
        ]
    scratch += [pltpu.VMEM((PLANES, rows, cols), F32)]
    scratch += [
        dma((4,)), dma((2,)), dma((2,)),
        dma((2, 2, PLANES)), dma((2, PLANES)), dma((2, 2, PLANES)), dma((2, PLANES)),
        dma((7,)), dma((7,)), dma((8,)), dma((8,)), dma((3,)), dma((3,)),
        dma((2,)), dma((2,)), dma((8,)), dma((8,)), dma((3, PLANES + 1)), dma((3, PLANES + 1)),
    ]
    return pl.pallas_call(
        layer_kernel,
        out_shape=jax.ShapeDtypeStruct((rows, width), BF16),
        in_specs=[vmem] * 6 + [hbm] * 4,
        out_specs=vmem,
        scratch_shapes=scratch,
        compiler_params=pltpu.CompilerParams(
            collective_id=0, has_side_effects=True, vmem_limit_bytes=60 * 1024 * 1024
        ),
    )(
        tokens, norm_gain.reshape(1, -1), gates.reshape(1, -1), expert_ids.reshape(1, -1),
        slots.reshape(1, -1), dropped.reshape(1, -1), res_in, res_out,
        expert_in.reshape(expert_in.shape[1:]), expert_out.reshape(expert_out.shape[1:]),
    )


def rms_norm(tokens, norm_gain):
    values = tokens.astype(jnp.float32)
    scale = lax.rsqrt(jnp.mean(values * values, axis=-1, keepdims=True) + 1e-06)
    return (values * scale * norm_gain).astype(jnp.bfloat16)


def on_device(
    tokens, norm_gain, gates, expert_ids, slots, dropped, res_in, res_out, expert_in, expert_out
):
    n_rep = lax.axis_size("rep")
    n_ep = lax.axis_size("ep")
    rows = tokens.shape[0]
    width = tokens.shape[1]
    cap = rows // n_ep
    normed = rms_norm(tokens, norm_gain)
    keep = 1 - dropped
    gathered, ids_all, slots_all, keep_all = (
        lax.all_gather(normed, "rep", axis=0, tiled=True),
        lax.all_gather(expert_ids, "rep", axis=0, tiled=True),
        lax.all_gather(slots, "rep", axis=0, tiled=True),
        lax.all_gather(keep, "rep", axis=0, tiled=True),
    )
    replica = jnp.arange(n_rep * rows, dtype=jnp.int32) // rows
    target = ids_all * (n_rep * cap) + replica * cap + slots_all
    places = jnp.arange(n_ep * n_rep * cap, dtype=jnp.int32)
    table = ((target[None, :] == places[:, None]) & (keep_all[None, :] == 1)).astype(jnp.bfloat16)
    buffer = (
        jnp.dot(table, gathered, preferred_element_type=jnp.float32)
        .astype(jnp.bfloat16)
        .reshape(n_ep, n_rep * cap, width)
    )
    block = lax.all_to_all(buffer, "ep", split_axis=0, concat_axis=0, tiled=True)
    flat = block.reshape(-1, width)
    hidden = jax.nn.gelu(
        jnp.dot(flat, expert_in[0], preferred_element_type=jnp.float32), approximate=True
    ).astype(jnp.bfloat16)
    result = jnp.dot(hidden, expert_out[0], preferred_element_type=jnp.float32)
    back = lax.all_to_all(
        result.reshape(block.shape[0], block.shape[1], width).astype(jnp.bfloat16),
        "ep",
        split_axis=0,
        concat_axis=0,
        tiled=True,
    ).astype(jnp.float32)
    picked = jnp.take(back.reshape(-1, width), jnp.where(keep_all == 1, target, 0), axis=0)
    partial_rows = jnp.where(keep_all[:, None] == 1, picked, 0.0)
    weight_in = lax.all_gather(res_in, "ep", axis=0, tiled=True)
    hidden = jax.nn.gelu(
        jnp.dot(gathered, weight_in, preferred_element_type=jnp.float32), approximate=True
    ).astype(jnp.bfloat16)
    weight_out = lax.all_gather(res_out, "ep", axis=1, tiled=True)
    res_branch = lax.psum_scatter(
        jnp.dot(hidden, weight_out, preferred_element_type=jnp.float32),
        "rep",
        scatter_dimension=0,
        tiled=True,
    )
    exp_branch = lax.psum_scatter(partial_rows, "rep", scatter_dimension=0, tiled=True)
    mixed = tokens.astype(jnp.float32) + res_branch + gates[:, None] * exp_branch
    return mixed.astype(jnp.bfloat16)


def solution(mesh):
    planes = mesh.shape["rep"] == 4 and mesh.shape["ep"] == 2 * PLANES
    return jax.shard_map(
        one_kernel if planes else on_device,
        mesh=mesh,
        in_specs=(
            P(("rep", "ep"), None),
            P(),
            P(("rep", "ep")),
            P(("rep", "ep")),
            P(("rep", "ep")),
            P(("rep", "ep")),
            P("ep", "rep"),
            P("rep", "ep"),
            P("ep", None, "rep"),
            P("ep", "rep", None),
        ),
        out_specs=P(("rep", "ep"), None),
        check_vma=False,
    )
```

```python
import jax
import jax.numpy as jnp
from jax import lax
from jax.experimental import pallas as pl
from jax.experimental.pallas import tpu as pltpu
from jax.sharding import PartitionSpec as P

F32 = jnp.float32
BF16 = jnp.bfloat16
PLANES = 4


def gelu(x):
    return x * (0.5 * (1.0 + jnp.tanh(0.7978845608028654 * (x + 0.044715 * (x * x * x)))))


def dot(a, b):
    return jnp.dot(a, b, preferred_element_type=F32)


def layer_kernel(
    tokens, gain, gates, ids, slots, dropped, res_in, res_out, exp_in, exp_out,
    out,
    w1, w2, ein, eout, normed, xrows, disp, ehid,
    er_send, er_keep, er_recv, ey_send, ey_keep, ey_recv, eb_send, back,
    rhid, pc_send, pc_keep, pc_recv, px_send, px_keep, px_recv, py_send, py_keep, py_recv,
    res,
    local_sem, wx_ssem, wx_rsem, w1_ssem, w1_rsem, w2_ssem, w2_rsem,
    n_ssem, n_rsem, d_ssem, d_rsem, x_ssem, x_rsem, e_ssem, e_rsem, b_ssem, b_rsem,
    r_ssem, r_rsem,
):
    rep, ep = lax.axis_index("rep"), lax.axis_index("ep")
    y, c = rep // 2, rep % 2
    z, x = ep // 2, ep % 2
    rows, width = tokens.shape
    n_ep = 2 * PLANES
    cap = rows // n_ep
    half = w1.shape[1]
    chunk = res_in.shape[0]
    cols = 2 * chunk

    def dev(r, e):
        return {"rep": r, "ep": e}

    core_dev = dev(rep + 1 - 2 * c, ep)
    y_dev = dev(rep + 2 - 4 * y, ep)
    x_dev = dev(rep, ep + 1 - 2 * x)
    up_dev, down_dev = dev(rep, ep + 2), dev(rep, ep - 2)

    def peer(k):
        return lax.rem(ep + k, n_ep)

    def remote(src, dst, ssem, rsem, device):
        return pltpu.make_async_remote_copy(
            src_ref=src, dst_ref=dst, send_sem=ssem, recv_sem=rsem,
            device_id=device, device_id_type=pl.DeviceIdType.MESH,
        )

    def arrived(dst, ssem, rsem):
        remote(dst, dst, ssem, rsem, core_dev).wait_recv()

    sent = []

    def send(src, dst, ssem, rsem, device):
        copy = remote(src, dst, ssem, rsem, device)
        copy.start()
        sent.append(copy)

    def at(i, n):
        return pl.ds(pl.multiple_of(i * n, n), n)

    barrier = pltpu.get_barrier_semaphore()
    for k in range(1, n_ep):
        pl.semaphore_signal(
            barrier, inc=1, device_id=dev(rep, peer(k)), device_id_type=pl.DeviceIdType.MESH
        )
    for device in (core_dev, y_dev):
        pl.semaphore_signal(barrier, inc=1, device_id=device, device_id_type=pl.DeviceIdType.MESH)

    own_w1 = pltpu.make_async_copy(res_in.at[:, at(x, half)], w1.at[at(ep, chunk), :], local_sem.at[0])
    own_w2 = pltpu.make_async_copy(
        res_out.at[at(x, half), :], w2.at[z, :, at(x, chunk)], local_sem.at[1]
    )
    load_in = pltpu.make_async_copy(exp_in, ein, local_sem.at[2])
    load_out = pltpu.make_async_copy(exp_out, eout, local_sem.at[3])
    for copy in (own_w1, own_w2, load_in, load_out):
        copy.start()

    pl.semaphore_wait(barrier, n_ep + 1)

    send(res_in.at[:, at(1 - x, half)], w1.at[at(ep, chunk), :], wx_ssem.at[0], wx_rsem.at[0], x_dev)

    def w1_at(s, h):
        return w1.at[at(2 * s + h, chunk), :]

    def w2_at(s, h):
        return w2.at[s, :, at(h, chunk)]

    inner = (z > 0) & (z < PLANES - 1)

    def line_copy(piece, ssem, rsem, s, h, way):
        device = down_dev if way else up_dev
        return remote(piece(s, h), piece(s, h), ssem.at[way, h, s], rsem.at[h, s], device)

    def line_start(piece, ssem, rsem, h):
        @pl.when(z < PLANES - 1)
        def _():
            line_copy(piece, ssem, rsem, z, h, 0).start()

        @pl.when(z > 0)
        def _():
            line_copy(piece, ssem, rsem, z, h, 1).start()

    def order(j):
        flip = z >= PLANES // 2
        mine = jnp.where(flip, PLANES - 1 - z, z)
        s = 1 - mine if j == 0 else j + 1
        return jnp.where(flip, PLANES - 1 - s, s)

    def line_wait(piece, ssem, rsem, j, halves=(0, 1)):
        s = order(j)

        @pl.when(jnp.logical_not(inner))
        def _():
            for h in halves:
                line_copy(piece, ssem, rsem, s, h, 0).wait_recv()

    def line_step(piece, ssem, rsem, j):
        s = order(j)
        for h in (0, 1):
            @pl.when(inner)
            def _():
                line_copy(piece, ssem, rsem, s, h, 0).wait_recv()

            @pl.when(inner & (s < z))
            def _():
                line_copy(piece, ssem, rsem, s, h, 0).start()

            @pl.when(inner & (s > z))
            def _():
                line_copy(piece, ssem, rsem, s, h, 1).start()

    def line_end(piece, ssem, rsem):
        for h in (0, 1):
            @pl.when(z < PLANES - 1)
            def _():
                line_copy(piece, ssem, rsem, z, h, 0).wait_send()

            @pl.when(z > 0)
            def _():
                line_copy(piece, ssem, rsem, z, h, 1).wait_send()

            for j in range(PLANES - 1):
                s = order(j)

                @pl.when(inner & (s < z))
                def _():
                    line_copy(piece, ssem, rsem, s, h, 0).wait_send()

                @pl.when(inner & (s > z))
                def _():
                    line_copy(piece, ssem, rsem, s, h, 1).wait_send()

    own_w1.wait()
    line_start(w1_at, w1_ssem, w1_rsem, x)

    values = tokens[...].astype(F32)
    scale = lax.rsqrt(jnp.mean(values * values, axis=-1, keepdims=True) + 1e-06)
    own_normed = (values * scale * gain[...]).astype(BF16)

    def n_at(cc, xx, yy):
        return normed.at[at(cc * 4 + xx * 2 + yy, rows), :]

    normed[at(c * 4 + x * 2 + y, rows), :] = own_normed

    target = ids[...] * cap + slots[...]
    places = lax.broadcasted_iota(jnp.int32, (n_ep * cap, rows), 0)
    table = jnp.where((places == target) & (dropped[...] == 0), 1.0, 0.0).astype(BF16)
    disp[...] = dot(table, own_normed).astype(BF16)

    def x_at(cc, yy):
        return xrows.at[at(cc * 2 + yy, rows), :]

    def x_part(cc, yy, e):
        return xrows.at[pl.ds(pl.multiple_of((cc * 2 + yy) * rows + e * cap, cap), cap), :]

    for k in range(1, n_ep):
        send(disp.at[at(peer(k), cap), :], x_part(c, y, ep), d_ssem.at[k], d_rsem.at[k], dev(rep, peer(k)))
    x_part(c, y, ep)[...] = disp[at(ep, cap), :]

    send(n_at(c, x, y), n_at(c, x, y), n_ssem.at[1], n_rsem.at[1], y_dev)
    send(n_at(c, x, y), n_at(c, x, y), n_ssem.at[2], n_rsem.at[2], core_dev)

    arrived(w1.at[at(ep + 1 - 2 * x, chunk), :], wx_ssem.at[0], wx_rsem.at[0])
    line_start(w1_at, w1_ssem, w1_rsem, 1 - x)
    own_w2.wait()
    line_start(w2_at, w2_ssem, w2_rsem, x)

    send(n_at(c, x, y), n_at(c, x, y), n_ssem.at[0], n_rsem.at[0], x_dev)
    send(
        res_out.at[at(1 - x, half), :], w2.at[z, :, at(x, chunk)],
        wx_ssem.at[1], wx_rsem.at[1], x_dev,
    )
    for k in range(1, n_ep):
        arrived(x_part(c, y, peer(n_ep - k)), d_ssem.at[k], d_rsem.at[k])
    send(x_at(c, y), x_at(c, y), x_ssem.at[0], x_rsem.at[0], y_dev)
    send(x_at(c, y), x_at(c, y), x_ssem.at[1], x_rsem.at[1], core_dev)
    arrived(n_at(c, x, 1 - y), n_ssem.at[1], n_rsem.at[1])
    send(n_at(c, x, 1 - y), n_at(c, x, 1 - y), n_ssem.at[5], n_rsem.at[5], core_dev)
    line_step(w1_at, w1_ssem, w1_rsem, 0)
    line_step(w1_at, w1_ssem, w1_rsem, 1)
    arrived(n_at(c, 1 - x, y), n_ssem.at[0], n_rsem.at[0])
    send(n_at(c, 1 - x, y), n_at(c, 1 - x, y), n_ssem.at[3], n_rsem.at[3], y_dev)
    send(n_at(c, 1 - x, y), n_at(c, 1 - x, y), n_ssem.at[4], n_rsem.at[4], core_dev)
    arrived(w2.at[z, :, at(1 - x, chunk)], wx_ssem.at[1], wx_rsem.at[1])
    line_start(w2_at, w2_ssem, w2_rsem, 1 - x)
    arrived(x_at(c, 1 - y), x_ssem.at[0], x_rsem.at[0])
    send(x_at(c, 1 - y), x_at(c, 1 - y), x_ssem.at[2], x_rsem.at[2], core_dev)
    line_step(w1_at, w1_ssem, w1_rsem, 2)

    arrived(x_at(1 - c, y), x_ssem.at[1], x_rsem.at[1])
    arrived(x_at(1 - c, 1 - y), x_ssem.at[2], x_rsem.at[2])
    load_in.wait()

    @pl.loop(0, ehid.shape[1] // 256)
    def _(i):
        ehid[:, at(i, 256)] = gelu(dot(xrows[...], ein[:, at(i, 256)])).astype(BF16)

    load_out.wait()

    @pl.loop(0, width // 256)
    def _(i):
        er_send[:, at(i, 256)] = dot(ehid[at(1 - c, 2 * rows), :], eout[:, at(i, 256)]).astype(BF16)
        er_keep[:, at(i, 256)] = dot(ehid[at(c, 2 * rows), :], eout[:, at(i, 256)])

    send(er_send, er_recv, e_ssem.at[0], e_rsem.at[0], core_dev)
    arrived(er_recv, e_ssem.at[0], e_rsem.at[0])
    ey_send[...] = (er_keep[at(1 - y, rows), :] + er_recv[at(1 - y, rows), :].astype(F32)).astype(BF16)
    send(ey_send, ey_recv, e_ssem.at[1], e_rsem.at[1], y_dev)
    ey_keep[...] = er_keep[at(y, rows), :] + er_recv[at(y, rows), :].astype(F32)

    arrived(n_at(c, 1 - x, 1 - y), n_ssem.at[3], n_rsem.at[3])
    send(n_at(c, 1 - x, 1 - y), n_at(c, 1 - x, 1 - y), n_ssem.at[6], n_rsem.at[6], core_dev)
    arrived(n_at(1 - c, x, y), n_ssem.at[2], n_rsem.at[2])
    arrived(n_at(1 - c, 1 - x, y), n_ssem.at[4], n_rsem.at[4])
    arrived(n_at(1 - c, x, 1 - y), n_ssem.at[5], n_rsem.at[5])
    arrived(n_at(1 - c, 1 - x, 1 - y), n_ssem.at[6], n_rsem.at[6])

    for j in range(PLANES - 1):
        line_wait(w1_at, w1_ssem, w1_rsem, j)

    @pl.loop(0, normed.shape[0] // 256)
    def _(i):
        rhid[at(i, 256), :] = gelu(dot(normed[at(i, 256), :], w1[...])).astype(BF16)

    def stage_a(s, q, cs):
        pc_send[s, :, cs] = dot(rhid[at(1 - c, 4 * rows), :], w2[s, :, cs]).astype(BF16)
        send(pc_send.at[s, :, cs], pc_recv.at[s, :, cs], r_ssem.at[0, q], r_rsem.at[0, q], core_dev)
        pc_keep[s, :, cs] = dot(rhid[at(c, 4 * rows), :], w2[s, :, cs])

    def stage_b(s, q, cs):
        arrived(pc_recv.at[s, :, cs], r_ssem.at[0, q], r_rsem.at[0, q])
        away, stay = at(1 - x, 2 * rows), at(x, 2 * rows)
        px_send[s, :, cs] = (pc_keep[s, away, cs] + pc_recv[s, away, cs].astype(F32)).astype(BF16)
        send(px_send.at[s, :, cs], px_recv.at[s, :, cs], r_ssem.at[1, q], r_rsem.at[1, q], x_dev)
        px_keep[s, :, cs] = pc_keep[s, stay, cs] + pc_recv[s, stay, cs].astype(F32)

    def stage_c(s, q, cs):
        arrived(px_recv.at[s, :, cs], r_ssem.at[1, q], r_rsem.at[1, q])
        away, stay = at(1 - y, rows), at(y, rows)
        py_send[s, :, cs] = (px_keep[s, away, cs] + px_recv[s, away, cs].astype(F32)).astype(BF16)
        send(py_send.at[s, :, cs], py_recv.at[s, :, cs], r_ssem.at[2, q], r_rsem.at[2, q], y_dev)
        py_keep[s, :, cs] = px_keep[s, stay, cs] + px_recv[s, stay, cs].astype(F32)

    def stage_d(s, q, cs):
        arrived(py_recv.at[s, :, cs], r_ssem.at[2, q], r_rsem.at[2, q])
        res[s, :, cs] = py_keep[s, :, cs] + py_recv[s, :, cs].astype(F32)

    s0, s1, s2, s3 = z, order(0), order(1), order(2)
    whole, left, right = pl.ds(0, cols), pl.ds(0, chunk), pl.ds(chunk, chunk)
    line_step(w2_at, w2_ssem, w2_rsem, 0)
    line_step(w2_at, w2_ssem, w2_rsem, 1)
    stage_a(s0, s0, whole)
    arrived(ey_recv, e_ssem.at[1], e_rsem.at[1])
    eb_send[...] = (ey_keep[...] + ey_recv[...].astype(F32)).astype(BF16)
    for k in range(1, n_ep):
        send(
            eb_send.at[at(peer(k), cap), :], back.at[at(ep, cap), :],
            b_ssem.at[k], b_rsem.at[k], dev(rep, peer(k)),
        )
    back[at(ep, cap), :] = eb_send[at(ep, cap), :]

    stage_b(s0, s0, whole)
    line_wait(w2_at, w2_ssem, w2_rsem, 0)
    stage_a(s1, s1, whole)
    stage_b(s1, s1, whole)
    line_step(w2_at, w2_ssem, w2_rsem, 2)
    stage_c(s0, s0, whole)
    line_wait(w2_at, w2_ssem, w2_rsem, 1)
    stage_a(s2, s2, whole)
    stage_b(s2, s2, whole)
    stage_c(s1, s1, whole)
    stage_d(s0, s0, whole)
    for k in range(1, n_ep):
        arrived(back.at[at(peer(n_ep - k), cap), :], b_ssem.at[k], b_rsem.at[k])
    same = lax.broadcasted_iota(jnp.int32, (rows, rows), 0) == lax.broadcasted_iota(
        jnp.int32, (rows, rows), 1
    )
    gate = jnp.sum(jnp.where(same, gates[...], 0.0), axis=1, keepdims=True)
    picked = lax.dot_general(
        table, back[...], (((0,), (0,)), ((), ())), preferred_element_type=F32
    )
    ey_keep[...] = tokens[...].astype(F32) + gate * picked

    stage_c(s2, s2, whole)
    stage_d(s1, s1, whole)
    line_wait(w2_at, w2_ssem, w2_rsem, 2, (0,))
    stage_a(s3, s3, left)
    stage_d(s2, s2, whole)
    stage_b(s3, s3, left)
    line_wait(w2_at, w2_ssem, w2_rsem, 2, (1,))
    stage_a(s3, PLANES, right)
    stage_b(s3, PLANES, right)
    stage_c(s3, s3, left)
    stage_c(s3, PLANES, right)
    stage_d(s3, s3, left)
    stage_d(s3, PLANES, right)
    for s in range(PLANES):
        columns = pl.ds(s * cols, cols)
        out[:, columns] = (ey_keep[:, columns] + res[s]).astype(BF16)

    for copy in sent:
        copy.wait_send()
    line_end(w1_at, w1_ssem, w1_rsem)
    line_end(w2_at, w2_ssem, w2_rsem)


def one_kernel(
    tokens, norm_gain, gates, expert_ids, slots, dropped, res_in, res_out, expert_in, expert_out
):
    rows, width = tokens.shape
    chunk = res_in.shape[0]
    half = res_in.shape[1] // 2
    cols = 2 * chunk
    units = expert_in.shape[2]
    vmem = pl.BlockSpec(memory_space=pltpu.VMEM)
    hbm = pl.BlockSpec(memory_space=pl.ANY)
    dma = pltpu.SemaphoreType.DMA
    scratch = [
        pltpu.VMEM((width, half), BF16),
        pltpu.VMEM((PLANES, half, cols), BF16),
        pltpu.VMEM((width, units), BF16),
        pltpu.VMEM((units, width), BF16),
        pltpu.VMEM((8 * rows, width), BF16),
        pltpu.VMEM((4 * rows, width), BF16),
        pltpu.VMEM((rows, width), BF16),
        pltpu.VMEM((4 * rows, units), BF16),
        pltpu.VMEM((2 * rows, width), BF16),
        pltpu.VMEM((2 * rows, width), F32),
        pltpu.VMEM((2 * rows, width), BF16),
        pltpu.VMEM((rows, width), BF16),
        pltpu.VMEM((rows, width), F32),
        pltpu.VMEM((rows, width), BF16),
        pltpu.VMEM((rows, width), BF16),
        pltpu.VMEM((rows, width), BF16),
        pltpu.VMEM((8 * rows, half), BF16),
    ]
    for part in (4, 2, 1):
        scratch += [
            pltpu.VMEM((PLANES, part * rows, cols), BF16),
            pltpu.VMEM((PLANES, part * rows, cols), F32),
            pltpu.VMEM((PLANES, part * rows, cols), BF16),
        ]
    scratch += [pltpu.VMEM((PLANES, rows, cols), F32)]
    scratch += [
        dma((4,)), dma((2,)), dma((2,)),
        dma((2, 2, PLANES)), dma((2, PLANES)), dma((2, 2, PLANES)), dma((2, PLANES)),
        dma((7,)), dma((7,)), dma((8,)), dma((8,)), dma((3,)), dma((3,)),
        dma((2,)), dma((2,)), dma((8,)), dma((8,)), dma((3, PLANES + 1)), dma((3, PLANES + 1)),
    ]
    return pl.pallas_call(
        layer_kernel,
        out_shape=jax.ShapeDtypeStruct((rows, width), BF16),
        in_specs=[vmem] * 6 + [hbm] * 4,
        out_specs=vmem,
        scratch_shapes=scratch,
        compiler_params=pltpu.CompilerParams(
            collective_id=0, has_side_effects=True, vmem_limit_bytes=60 * 1024 * 1024
        ),
    )(
        tokens, norm_gain.reshape(1, -1), gates.reshape(1, -1), expert_ids.reshape(1, -1),
        slots.reshape(1, -1), dropped.reshape(1, -1), res_in, res_out,
        expert_in.reshape(expert_in.shape[1:]), expert_out.reshape(expert_out.shape[1:]),
    )


def rms_norm(tokens, norm_gain):
    values = tokens.astype(jnp.float32)
    scale = lax.rsqrt(jnp.mean(values * values, axis=-1, keepdims=True) + 1e-06)
    return (values * scale * norm_gain).astype(jnp.bfloat16)


def on_device(
    tokens, norm_gain, gates, expert_ids, slots, dropped, res_in, res_out, expert_in, expert_out
):
    n_rep = lax.axis_size("rep")
    n_ep = lax.axis_size("ep")
    rows = tokens.shape[0]
    width = tokens.shape[1]
    cap = rows // n_ep
    normed = rms_norm(tokens, norm_gain)
    keep = 1 - dropped
    gathered, ids_all, slots_all, keep_all = (
        lax.all_gather(normed, "rep", axis=0, tiled=True),
        lax.all_gather(expert_ids, "rep", axis=0, tiled=True),
        lax.all_gather(slots, "rep", axis=0, tiled=True),
        lax.all_gather(keep, "rep", axis=0, tiled=True),
    )
    replica = jnp.arange(n_rep * rows, dtype=jnp.int32) // rows
    target = ids_all * (n_rep * cap) + replica * cap + slots_all
    places = jnp.arange(n_ep * n_rep * cap, dtype=jnp.int32)
    table = ((target[None, :] == places[:, None]) & (keep_all[None, :] == 1)).astype(jnp.bfloat16)
    buffer = (
        jnp.dot(table, gathered, preferred_element_type=jnp.float32)
        .astype(jnp.bfloat16)
        .reshape(n_ep, n_rep * cap, width)
    )
    block = lax.all_to_all(buffer, "ep", split_axis=0, concat_axis=0, tiled=True)
    flat = block.reshape(-1, width)
    hidden = jax.nn.gelu(
        jnp.dot(flat, expert_in[0], preferred_element_type=jnp.float32), approximate=True
    ).astype(jnp.bfloat16)
    result = jnp.dot(hidden, expert_out[0], preferred_element_type=jnp.float32)
    back = lax.all_to_all(
        result.reshape(block.shape[0], block.shape[1], width).astype(jnp.bfloat16),
        "ep",
        split_axis=0,
        concat_axis=0,
        tiled=True,
    ).astype(jnp.float32)
    picked = jnp.take(back.reshape(-1, width), jnp.where(keep_all == 1, target, 0), axis=0)
    partial_rows = jnp.where(keep_all[:, None] == 1, picked, 0.0)
    weight_in = lax.all_gather(res_in, "ep", axis=0, tiled=True)
    hidden = jax.nn.gelu(
        jnp.dot(gathered, weight_in, preferred_element_type=jnp.float32), approximate=True
    ).astype(jnp.bfloat16)
    weight_out = lax.all_gather(res_out, "ep", axis=1, tiled=True)
    res_branch = lax.psum_scatter(
        jnp.dot(hidden, weight_out, preferred_element_type=jnp.float32),
        "rep",
        scatter_dimension=0,
        tiled=True,
    )
    exp_branch = lax.psum_scatter(partial_rows, "rep", scatter_dimension=0, tiled=True)
    mixed = tokens.astype(jnp.float32) + res_branch + gates[:, None] * exp_branch
    return mixed.astype(jnp.bfloat16)


def solution(mesh):
    planes = mesh.shape["rep"] == 4 and mesh.shape["ep"] == 2 * PLANES
    return jax.shard_map(
        one_kernel if planes else on_device,
        mesh=mesh,
        in_specs=(
            P(("rep", "ep"), None),
            P(),
            P(("rep", "ep")),
            P(("rep", "ep")),
            P(("rep", "ep")),
            P(("rep", "ep")),
            P("ep", "rep"),
            P("rep", "ep"),
            P("ep", None, "rep"),
            P("ep", "rep", None),
        ),
        out_specs=P(("rep", "ep"), None),
        check_vma=False,
    )
```
